32 devices in a mesh: pre: 8 (over y, x, core), rep: 4 (over z).
Axes of the slice: x: 2, y: 2, z: 4, core: 2. Of those that a mesh axis runs over, the one named last changes fastest.
Arguments:
- grads: bfloat16 [8, 8, 512, 512], P('rep', 'pre')
- owner: int32 [8], replicated, may hold values from 0 to 7, as said below
- state: float32 [8, 2, 512, 512], P('pre', None, 'rep'), as said below
Outputs:
- new_state: float32 [8, 2, 512, 512], P('pre', None, 'rep')
- update: bfloat16 [8, 512, 512], P('pre', 'rep')
The draws below stay inside these ranges and needn't reach their ends.
Inputs may be any that keep to these rules, and one draw needn't show every extreme that they name: Each owner index is named by at most 2 blocks, and some owner by exactly 2. `state`: each matrix is symmetric.
All inputs are finite; a program needn't handle non-finite values.
Results may differ from the reference program's by a relative error of at most 0.006.
Values sent between devices are 32-bit elements; how exact they have to be, the bound alone decides.
A program may use at most 64 MiB of HBM per device.

```python
import math
import jax
import jax.numpy as jnp
from jax import lax

K = 512
CAP = 2
ITERS = 4
NB = 8
SHARDS = 8
N_PRE = 8


def draw_grads(key, part):
    key = jax.random.fold_in(key, 11)
    keys = jax.random.split(key, 3)
    row_scale = jnp.exp(jax.random.uniform(keys[0], (1, NB, K, 1)) * math.log(10.0))
    shard_scale = 3.0 ** (jnp.arange(SHARDS, dtype=jnp.float32) / (SHARDS - 1))
    common = jax.random.normal(keys[1], (1, NB, K, K))
    noise = jax.random.normal(keys[2], (SHARDS, NB, K, K))
    values = 3.0 * row_scale * (common + shard_scale[:, None, None, None] * noise)
    return values.astype(jnp.bfloat16)


def draw_owner(key, part):
    key = jax.random.fold_in(key, 17)
    keys = jax.random.split(key, 2)
    first = jax.random.randint(keys[0], (), 0, N_PRE).astype(jnp.int32)
    shared = (first + N_PRE - 1) % N_PRE
    second = (first + 1) % N_PRE
    others = (shared + 1 + jnp.arange(N_PRE - 1, dtype=jnp.int32)) % N_PRE
    others = others[jax.random.permutation(keys[1], N_PRE - 1)]
    rest = (first + 2 + jnp.arange(N_PRE - 2, dtype=jnp.int32)) % N_PRE
    result = jnp.zeros((NB,), jnp.int32)
    result = result.at[rest].set(others[:N_PRE - 2])
    result = result.at[first].set(shared)
    result = result.at[second].set(shared)
    return result


def draw_state(key, part):
    key = jax.random.fold_in(key, 23)
    keys = jax.random.split(key, 3)
    spread = jax.random.uniform(keys[0], (N_PRE, CAP, K))
    base = 10.0 * K * SHARDS
    position = jnp.arange(K, dtype=jnp.float32) / (K - 1)
    diagonal = base * jnp.exp(spread * math.log(100.0)) * 3.0 ** position
    places = jax.random.uniform(keys[1], (N_PRE, CAP, K)) * K
    signs = (2 * jax.random.randint(keys[2], (N_PRE, CAP, K), 0, 2) - 1).astype(jnp.float32)
    kernel = jnp.exp(-jnp.abs(places[..., :, None] - places[..., None, :]) / 8.0)
    coupling = signs[..., :, None] * signs[..., None, :] * kernel
    rooted = jnp.sqrt(diagonal)
    identity = jnp.eye(K, dtype=jnp.float32)
    return rooted[..., :, None] * rooted[..., None, :] * (identity + 0.8 * coupling)


def setup_inputs(seed: int = 0) -> dict:
    arg_keys = jax.random.split(jax.random.key(seed), 4)
    return {
        "grads": draw_grads(jax.random.fold_in(arg_keys[3], 71), 0),
        "owner": draw_owner(jax.random.fold_in(arg_keys[3], 71), 0),
        "state": draw_state(jax.random.fold_in(arg_keys[3], 71), 0),
    }


DAMP = 0.05

def root_iterate(stat):
    order_size = stat.shape[0]
    identity = jnp.eye(order_size, dtype=jnp.float32)
    norm_stat = jnp.sqrt(jnp.sum(stat * stat))
    damped = stat + DAMP * norm_stat * identity
    scale_norm = jnp.sqrt(jnp.sum(damped * damped))
    iterate = damped / scale_norm
    root_block = scale_norm ** (-0.25) * identity
    for rounds in range(ITERS):
        factor = (5.0 * identity - iterate) * 0.25
        root_block = jnp.dot(root_block, factor, precision=lax.Precision.HIGHEST)
        if rounds + 1 < ITERS:
            for repeat in range(4):
                iterate = jnp.dot(iterate, factor, precision=lax.Precision.HIGHEST)
    return root_block

def reference(grads, owner, state):
    block_ids = jnp.arange(NB, dtype=jnp.int32)
    earlier = (owner[None, :] == owner[:, None]) & (block_ids[None, :] < block_ids[:, None])
    slot_of = lax.optimization_barrier(jnp.sum(earlier.astype(jnp.int32), axis=1))

    def gram_of(block_id):
        shards = lax.dynamic_index_in_dim(grads, block_id, 1, keepdims=False)
        return lax.dot_general(shards, shards, (((0, 2), (0, 2)), ((), ())), preferred_element_type=jnp.float32)
    gram_all = lax.map(gram_of, block_ids)
    owner_ids = jnp.arange(N_PRE, dtype=jnp.int32)
    slot_ids = jnp.arange(CAP, dtype=jnp.int32)
    select = ((owner[None, None, :] == owner_ids[:, None, None]) & (slot_of[None, None, :] == slot_ids[None, :, None])).astype(jnp.float32)
    new_state = state + jnp.einsum('osb,bij->osij', select, gram_all, precision=lax.Precision.HIGHEST)
    stat_all = new_state[owner, slot_of]
    root_all = lax.map(root_iterate, stat_all)

    def apply_block(block_id):
        shards = lax.dynamic_index_in_dim(grads, block_id, 1, keepdims=False)
        mean_grad = (lax.optimization_barrier(jnp.sum(shards.astype(jnp.float32), axis=0)) / SHARDS).astype(jnp.bfloat16)
        precond = lax.dynamic_index_in_dim(root_all, block_id, 0, keepdims=False).astype(jnp.bfloat16)
        return jnp.dot(precond, mean_grad, preferred_element_type=jnp.float32).astype(jnp.bfloat16)
    update = lax.map(apply_block, block_ids)
    return (new_state, update)
```

```python
import functools

import jax
import jax.numpy as jnp
from jax import lax
from jax.experimental import pallas as pl
from jax.experimental.pallas import tpu as pltpu
from jax.sharding import PartitionSpec as P

DAMP = 0.05
LANES = 128
LAG = 2
CENTER = 1.5625


def nt_dot(a, b):
    return lax.dot_general(a, b, (((1,), (1,)), ((), ())), preferred_element_type=jnp.float32)


def dot(a, b):
    return jnp.dot(a, b, preferred_element_type=jnp.float32)


def kernel(
    n_pre,
    n_rep,
    owner_ref,
    grads_ref,
    state_ref,
    new_state_ref,
    update_ref,
    loc,
    up,
    dn,
    tot,
    route_out,
    route_in,
    rows_in,
    stat,
    mean,
    x_f32,
    x_b16,
    e_f32,
    e_b16,
    g_b16,
    in_send,
    out_send,
    up_recv,
    dn_recv,
    route_send,
    route_recv,
    rows_send,
    rows_recv,
):
    pre, rep = lax.axis_index("pre"), lax.axis_index("rep")
    shards, order = grads_ref.shape[0], grads_ref.shape[2]
    rows, capacity = state_ref.shape[2], state_ref.shape[1]
    blocks = order // LANES
    half = n_rep // 2
    is_end = (rep == 0) | (rep == n_rep - 1)
    is_mid = (rep == half - 1) | (rep == half)
    not_end, not_mid = jnp.logical_not(is_end), jnp.logical_not(is_mid)
    inward = jnp.where(rep < half, rep + 1, rep - 1)
    outward = jnp.where(rep < half, rep - 1, rep + 1)

    mean_tiles = [(i, j) for i in range(n_rep) for j in range(blocks)]
    stat_tiles = [(i, j) for i in range(n_rep) for j in range(i * rows // LANES, blocks)]
    n_mean, total = len(mean_tiles), len(mean_tiles) + len(stat_tiles)

    def remote(src, dst, send, recv, device):
        return pltpu.make_async_remote_copy(
            src_ref=src,
            dst_ref=dst,
            send_sem=send,
            recv_sem=recv,
            device_id=device,
            device_id_type=pl.DeviceIdType.MESH,
        )

    barrier = pltpu.get_barrier_semaphore()

    @pl.loop(1, n_pre)
    def _(step):
        pl.semaphore_signal(
            barrier,
            inc=1,
            device_id={"pre": lax.rem(pre + step, n_pre)},
            device_id_type=pl.DeviceIdType.MESH,
        )

    pl.semaphore_signal(
        barrier, inc=1, device_id={"rep": inward}, device_id_type=pl.DeviceIdType.MESH
    )

    @pl.when(not_end)
    def _():
        pl.semaphore_signal(
            barrier, inc=1, device_id={"rep": outward}, device_id_type=pl.DeviceIdType.MESH
        )

    pl.semaphore_wait(barrier, jnp.where(is_end, n_pre, n_pre + 1))

    def slot_of(block):
        mine = owner_ref[block]

        def count(other, found):
            same = (owner_ref[other] == mine) & (other < block)
            return found + same.astype(jnp.int32)

        return lax.fori_loop(0, n_pre, count, jnp.int32(0))

    def piece(block):
        return state_ref[0, jnp.minimum(slot_of(block), capacity - 1)]

    def route_copy(step):
        peer = lax.rem(pre + step, n_pre)
        return remote(
            route_out.at[step],
            route_in.at[pre],
            route_send.at[step],
            route_recv.at[step],
            {"pre": peer},
        )

    @pl.loop(1, n_pre)
    def _(step):
        route_out[step] = piece(lax.rem(pre + step, n_pre))
        route_copy(step).start()

    route_in[pre] = piece(pre)

    def send_in(k):
        @pl.when(is_mid)
        def _():
            remote(
                loc.at[k], dn.at[k], in_send.at[k], dn_recv.at[k], {"rep": inward}
            ).start()

        @pl.when(not_mid)
        def _():
            remote(
                loc.at[k], up.at[k], in_send.at[k], up_recv.at[k], {"rep": inward}
            ).start()

    def out_copy(k):
        return remote(tot.at[k], dn.at[k], out_send.at[k], dn_recv.at[k], {"rep": outward})

    def in_copy(k):
        return remote(loc.at[k], up.at[k], in_send.at[k], up_recv.at[k], {"rep": inward})

    def step_up(k):
        @pl.when(not_end)
        def _():
            in_copy(k).wait_recv()
            loc[k] = loc[k] + up[k]
            send_in(k)

    def step_down(k):
        out_copy(k).wait_recv()

        @pl.when(is_mid)
        def _():
            tot[k] = loc[k] + dn[k]

        @pl.when(not_mid)
        def _():
            tot[k] = dn[k]

        @pl.when(not_end)
        def _():
            out_copy(k).start()

    for k, (i, j) in enumerate(mean_tiles):
        r, c = slice(i * rows, (i + 1) * rows), slice(j * LANES, (j + 1) * LANES)
        acc = grads_ref[0, 0, r, c].astype(jnp.float32)
        for s in range(1, shards):
            acc = acc + grads_ref[s, 0, r, c].astype(jnp.float32)
        loc[k] = acc

        @pl.when(is_end)
        def _():
            send_in(k)

    for a in range(blocks):
        low = a * LANES
        gram = nt_dot(grads_ref[0, 0, low : low + LANES, :], grads_ref[0, 0, low:, :])
        for s in range(1, shards):
            gram = gram + nt_dot(grads_ref[s, 0, low : low + LANES, :], grads_ref[s, 0, low:, :])
        for k, (i, j) in enumerate(stat_tiles):
            if i * rows // LANES == a:
                r = i * rows - low
                loc[n_mean + k] = gram[r : r + rows, j * LANES - low : (j + 1) * LANES - low]

    def inject():
        @pl.loop(1, n_pre)
        def _(step):
            route_copy(step).wait_recv()

        held = route_in[owner_ref[pre]]
        for k, (i, j) in enumerate(stat_tiles):

            @pl.when(rep == i)
            def _():
                loc[n_mean + k] = loc[n_mean + k] + held[:, j * LANES : (j + 1) * LANES]

    @pl.when(is_end)
    def _():
        inject()

        @pl.loop(n_mean, total)
        def _(k):
            send_in(k)

    @pl.loop(0, LAG)
    def _(k):
        step_up(k)

    @pl.loop(LAG, n_mean)
    def _(k):
        step_up(k)
        step_down(k - LAG)

    @pl.when(not_end)
    def _():
        inject()

    @pl.loop(n_mean, total)
    def _(k):
        step_up(k)
        step_down(k - LAG)

    @pl.loop(total - LAG, total)
    def _(k):
        step_down(k)

    for k, (i, j) in enumerate(stat_tiles):
        stat[i * rows : (i + 1) * rows, j * LANES : (j + 1) * LANES] = tot[n_mean + k]
    for a in range(blocks):
        for b in range(a + 1, blocks):
            ra, rb = slice(a * LANES, (a + 1) * LANES), slice(b * LANES, (b + 1) * LANES)
            stat[rb, ra] = stat[ra, rb].T

    start = pl.multiple_of(rep * rows, rows)

    def rows_copy(step):
        peer = lax.rem(pre + step, n_pre)
        return remote(
            stat.at[pl.ds(start, rows)],
            rows_in.at[pre],
            rows_send.at[step],
            rows_recv.at[step],
            {"pre": peer},
        )

    @pl.loop(1, n_pre)
    def _(step):
        rows_copy(step).start()

    rows_in[pre] = stat[pl.ds(start, rows), :]

    for k, (i, j) in enumerate(mean_tiles):
        mean[i * rows : (i + 1) * rows, j * LANES : (j + 1) * LANES] = (
            tot[k] / (shards * n_rep)
        ).astype(jnp.bfloat16)

    def eye(first, count):
        r = lax.broadcasted_iota(jnp.int32, (count, order), 0) + first
        c = lax.broadcasted_iota(jnp.int32, (count, order), 1)
        return (r == c).astype(jnp.float32)

    bands = range(0, order, 256)
    squares = jnp.zeros((1, 1), jnp.float32)
    for b in bands:
        part = stat[b : b + 256, :]
        squares = squares + jnp.sum(part * part, keepdims=True)
    shift = DAMP * jnp.sqrt(squares)
    squares = jnp.zeros((1, 1), jnp.float32)
    for b in bands:
        part = stat[b : b + 256, :] + shift * eye(b, 256)
        x_f32[b : b + 256, :] = part
        squares = squares + jnp.sum(part * part, keepdims=True)
    scale = jnp.sqrt(squares)
    for b in bands:
        part = x_f32[b : b + 256, :] / scale
        x_f32[b : b + 256, :] = part
        x_b16[b : b + 256, :] = part.astype(jnp.bfloat16)
    root = (1.25 * eye(start, rows) - 0.25 * x_f32[pl.ds(start, rows), :]) / jnp.sqrt(
        jnp.sqrt(scale)
    )

    def quadratic(b):
        square = dot(x_b16[pl.ds(b, 256), :], x_b16[...])
        return 0.0625 * square - 0.625 * x_f32[pl.ds(b, 256), :]

    @pl.loop(0, 2, init_carry=root)
    def root(_, root):
        @pl.loop(0, order, step=256)
        def _(b):
            e = quadratic(b)
            e_f32[pl.ds(b, 256), :] = e
            e_b16[pl.ds(b, 256), :] = e.astype(jnp.bfloat16)

        @pl.loop(0, order, step=256)
        def _(b):
            g = 2.0 * CENTER * e_f32[pl.ds(b, 256), :] + dot(e_b16[pl.ds(b, 256), :], e_b16[...])
            g_b16[pl.ds(b, 256), :] = g.astype(jnp.bfloat16)

        @pl.loop(0, order, step=256)
        def _(b):
            x = CENTER * CENTER * x_f32[pl.ds(b, 256), :] + dot(
                x_b16[pl.ds(b, 256), :], g_b16[...]
            )
            x_f32[pl.ds(b, 256), :] = x
            x_b16[pl.ds(b, 256), :] = x.astype(jnp.bfloat16)

        return 1.25 * root - 0.25 * dot(root.astype(jnp.bfloat16), x_b16[...])

    @pl.loop(0, order, step=256)
    def _(b):
        e_b16[pl.ds(b, 256), :] = quadratic(b).astype(jnp.bfloat16)

    last = dot(root.astype(jnp.bfloat16), x_b16[...])
    for _ in range(2):
        last = CENTER * last + dot(last.astype(jnp.bfloat16), e_b16[...])
    precond = (1.25 * root - 0.25 * last).astype(jnp.bfloat16)
    update_ref[0] = dot(precond, mean[...]).astype(jnp.bfloat16)

    @pl.loop(1, n_pre)
    def _(step):
        rows_copy(step).wait_recv()

    for j in range(capacity):

        def find(block, found):
            has, at = found
            here = ((owner_ref[block] == pre) & (slot_of(block) == j)).astype(jnp.int32)
            return has + here, at + here * block

        has, at = lax.fori_loop(0, n_pre, find, (jnp.int32(0), jnp.int32(0)))
        taken = jnp.full((rows, order), has, jnp.int32) > 0
        new_state_ref[0, j] = jnp.where(taken, rows_in[at], state_ref[0, j])

    @pl.loop(1, n_pre)
    def _(step):
        route_copy(step).wait_send()
        rows_copy(step).wait_send()

    @pl.loop(0, total)
    def _(k):
        in_copy(k).wait_send()

        @pl.when(not_end)
        def _():
            out_copy(k).wait_send()


def body(n_pre, n_rep, grads, owner, state):
    order = grads.shape[2]
    rows = state.shape[2]
    blocks = order // LANES
    total = n_rep * blocks + sum(blocks - i * rows // LANES for i in range(n_rep))
    f32, b16 = jnp.float32, jnp.bfloat16
    dma = pltpu.SemaphoreType.DMA
    vmem = pl.BlockSpec(memory_space=pltpu.VMEM)
    return pl.pallas_call(
        functools.partial(kernel, n_pre, n_rep),
        out_shape=(
            jax.ShapeDtypeStruct(state.shape, f32),
            jax.ShapeDtypeStruct((1, rows, order), b16),
        ),
        in_specs=[pl.BlockSpec(memory_space=pltpu.SMEM), vmem, vmem],
        out_specs=(vmem, vmem),
        scratch_shapes=[pltpu.VMEM((total, rows, LANES), f32)] * 4
        + [pltpu.VMEM((n_pre, rows, order), f32)] * 3
        + [pltpu.VMEM((order, order), t) for t in (f32, b16, f32, b16, f32, b16, b16)]
        + [dma((total,))] * 4
        + [dma((n_pre,))] * 4,
        compiler_params=pltpu.CompilerParams(
            collective_id=0, has_side_effects=True, vmem_limit_bytes=40 * 1024 * 1024
        ),
        cost_estimate=pl.CostEstimate(
            flops=20 * order**3, bytes_accessed=4 * order * order * 4, transcendentals=0
        ),
    )(owner, grads, state)


def solution(mesh):
    placed = (P("rep", "pre", None, None), P(), P("pre", None, "rep", None))
    return jax.shard_map(
        functools.partial(body, mesh.shape["pre"], mesh.shape["rep"]),
        mesh=mesh,
        in_specs=placed,
        out_specs=(P("pre", None, "rep", None), P("pre", "rep", None)),
        check_vma=False,
    )
```

```python
import functools

import jax
import jax.numpy as jnp
from jax import lax
from jax.experimental import pallas as pl
from jax.experimental.pallas import tpu as pltpu
from jax.sharding import PartitionSpec as P

DAMP = 0.05
LANES = 128
LAG = 3
CENTER = 1.5625


def nt_dot(a, b):
    return lax.dot_general(a, b, (((1,), (1,)), ((), ())), preferred_element_type=jnp.float32)


def dot(a, b):
    return jnp.dot(a, b, preferred_element_type=jnp.float32)


def kernel(
    n_pre,
    n_rep,
    owner_ref,
    grads_ref,
    state_ref,
    new_state_ref,
    update_ref,
    loc,
    up,
    dn,
    tot,
    core_out,
    core_in,
    route_out,
    route_in,
    rows_in,
    stat,
    mean,
    x_f32,
    x_b16,
    e_f32,
    e_b16,
    g_b16,
    in_send,
    out_send,
    up_recv,
    dn_recv,
    core_send,
    core_recv,
    route_send,
    route_recv,
    rows_send,
    rows_recv,
    pass_send,
    pass_recv,
):
    pre, rep = lax.axis_index("pre"), lax.axis_index("rep")
    shards, order = grads_ref.shape[0], grads_ref.shape[2]
    rows, capacity = state_ref.shape[2], state_ref.shape[1]
    blocks = order // LANES
    half = n_rep // 2
    is_end = (rep == 0) | (rep == n_rep - 1)
    is_mid = (rep == half - 1) | (rep == half)
    not_end, not_mid = jnp.logical_not(is_end), jnp.logical_not(is_mid)
    inward = jnp.where(rep < half, rep + 1, rep - 1)
    outward = jnp.where(rep < half, rep - 1, rep + 1)
    chips, chip, core = n_pre // 2, pre // 2, pre % 2
    partner = pre + 1 - 2 * core

    def chip_at(d):
        other, bit = chip, 1
        while bit < chips:
            if d & bit:
                other = other + bit * (1 - 2 * ((chip // bit) % 2))
            bit *= 2
        return other

    mean_tiles = [(i, j) for i in range(n_rep) for j in range(blocks)]
    stat_tiles = [(i, j) for i in range(n_rep) for j in range(i * rows // LANES, blocks)]
    early = len(mean_tiles) // 2
    after = early + len(stat_tiles)
    total = len(mean_tiles) + len(stat_tiles)

    def mean_place(k):
        return k if k < early else k + len(stat_tiles)

    def remote(src, dst, send, recv, device):
        return pltpu.make_async_remote_copy(
            src_ref=src,
            dst_ref=dst,
            send_sem=send,
            recv_sem=recv,
            device_id=device,
            device_id_type=pl.DeviceIdType.MESH,
        )

    barrier = pltpu.get_barrier_semaphore()

    def greet(device):
        pl.semaphore_signal(
            barrier, inc=1, device_id=device, device_id_type=pl.DeviceIdType.MESH
        )

    for d in range(1, chips):
        greet({"pre": 2 * chip_at(d) + core})
    greet({"pre": partner})
    greet({"rep": inward})

    @pl.when(not_end)
    def _():
        greet({"rep": outward})

    pl.semaphore_wait(barrier, jnp.where(is_end, chips + 1, chips + 2))

    def send_in(k):
        @pl.when(is_mid)
        def _():
            remote(
                loc.at[k], dn.at[k], in_send.at[k], dn_recv.at[k], {"rep": inward}
            ).start()

        @pl.when(not_mid)
        def _():
            remote(
                loc.at[k], up.at[k], in_send.at[k], up_recv.at[k], {"rep": inward}
            ).start()

    def out_copy(k):
        return remote(tot.at[k], dn.at[k], out_send.at[k], dn_recv.at[k], {"rep": outward})

    def in_copy(k):
        return remote(loc.at[k], up.at[k], in_send.at[k], up_recv.at[k], {"rep": inward})

    def step_up(k):
        @pl.when(not_end)
        def _():
            in_copy(k).wait_recv()
            loc[k] = loc[k] + up[k]
            send_in(k)

    def step_down(k):
        out_copy(k).wait_recv()

        @pl.when(is_mid)
        def _():
            tot[k] = loc[k] + dn[k]

        @pl.when(not_mid)
        def _():
            tot[k] = dn[k]

        @pl.when(not_end)
        def _():
            out_copy(k).start()

    for k, (i, j) in enumerate(mean_tiles):
        r, c = slice(i * rows, (i + 1) * rows), slice(j * LANES, (j + 1) * LANES)
        acc = grads_ref[0, 0, r, c].astype(jnp.float32)
        for s in range(1, shards):
            acc = acc + grads_ref[s, 0, r, c].astype(jnp.float32)
        loc[mean_place(k)] = acc
        if k < early:

            @pl.when(is_end)
            def _():
                send_in(k)

    def slot_of(block):
        mine = owner_ref[block]

        def count(other, found):
            same = (owner_ref[other] == mine) & (other < block)
            return found + same.astype(jnp.int32)

        return lax.fori_loop(0, n_pre, count, jnp.int32(0))

    def piece(block):
        return state_ref[0, jnp.minimum(slot_of(block), capacity - 1)]

    def core_copy(d):
        return remote(
            core_out.at[d], core_in.at[d], core_send.at[d], core_recv.at[d], {"pre": partner}
        )

    def route_copy(d):
        return remote(
            route_out.at[d],
            route_in.at[chip],
            route_send.at[d],
            route_recv.at[d],
            {"pre": 2 * chip_at(d) + core},
        )

    far_first = list(range(chips - 1, -1, -1))
    for d in far_first:
        core_out[d] = piece(2 * chip_at(d) + 1 - core)
        core_copy(d).start()

    for a in range(blocks):
        low = a * LANES
        gram = nt_dot(grads_ref[0, 0, low : low + LANES, :], grads_ref[0, 0, low:, :])
        for s in range(1, shards):
            gram = gram + nt_dot(grads_ref[s, 0, low : low + LANES, :], grads_ref[s, 0, low:, :])
        for k, (i, j) in enumerate(stat_tiles):
            if i * rows // LANES == a:
                r = i * rows - low
                loc[early + k] = gram[r : r + rows, j * LANES - low : (j + 1) * LANES - low]

    for d in far_first:
        block = 2 * chip_at(d) + core
        core_copy(d).wait_recv()
        theirs = jnp.full((rows, order), (owner_ref[block] == partner).astype(jnp.int32)) > 0
        chosen = jnp.where(theirs, core_in[d], piece(block))
        if d:
            route_out[d] = chosen
            route_copy(d).start()
        else:
            route_in[chip] = chosen

    def inject():
        for d in range(1, chips):
            route_copy(d).wait_recv()
        held = route_in[owner_ref[pre] // 2]
        for k, (i, j) in enumerate(stat_tiles):

            @pl.when(rep == i)
            def _():
                loc[early + k] = loc[early + k] + held[:, j * LANES : (j + 1) * LANES]

    @pl.when(is_end)
    def _():
        inject()

        @pl.loop(early, total)
        def _(k):
            send_in(k)

    @pl.loop(0, LAG)
    def _(k):
        step_up(k)

    @pl.loop(LAG, early)
    def _(k):
        step_up(k)
        step_down(k - LAG)

    @pl.when(not_end)
    def _():
        inject()

    @pl.loop(early, after + LAG)
    def _(k):
        step_up(k)
        step_down(k - LAG)

    def pump(part, parts=10):
        left = total - after
        for k in range(left * part // parts, left * (part + 1) // parts):
            if after + LAG + k < total:
                step_up(after + LAG + k)
            step_down(after + k)

    for k, (i, j) in enumerate(stat_tiles):
        stat[i * rows : (i + 1) * rows, j * LANES : (j + 1) * LANES] = tot[early + k]
    for a in range(blocks):
        for b in range(a + 1, blocks):
            ra, rb = slice(a * LANES, (a + 1) * LANES), slice(b * LANES, (b + 1) * LANES)
            stat[rb, ra] = stat[ra, rb].T

    start = pl.multiple_of(rep * rows, rows)

    def rows_copy(d):
        device = {"pre": 2 * chip_at(d) + core} if d else {"pre": partner}
        return remote(
            stat.at[pl.ds(start, rows)],
            rows_in.at[pre],
            rows_send.at[d],
            rows_recv.at[d],
            device,
        )

    def pass_copy(d):
        held = rows_in.at[2 * chip_at(d) + core]
        return remote(held, held, pass_send.at[d], pass_recv.at[d], {"pre": partner})

    def pass_on(d):
        rows_copy(d).wait_recv()
        pass_copy(d).start()

    for d in range(1, chips):
        rows_copy(d).start()
    rows_copy(0).start()
    rows_in[pre] = stat[pl.ds(start, rows), :]
    pump(0)

    def eye(first, count):
        r = lax.broadcasted_iota(jnp.int32, (count, order), 0) + first
        c = lax.broadcasted_iota(jnp.int32, (count, order), 1)
        return (r == c).astype(jnp.float32)

    bands = range(0, order, 256)
    squares = jnp.zeros((1, 1), jnp.float32)
    for b in bands:
        part = stat[b : b + 256, :]
        squares = squares + jnp.sum(part * part, keepdims=True)
    shift = DAMP * jnp.sqrt(squares)
    squares = jnp.zeros((1, 1), jnp.float32)
    for b in bands:
        part = stat[b : b + 256, :] + shift * eye(b, 256)
        x_f32[b : b + 256, :] = part
        squares = squares + jnp.sum(part * part, keepdims=True)
    scale = jnp.sqrt(squares)
    pump(1)
    for b in bands:
        part = x_f32[b : b + 256, :] / scale
        x_f32[b : b + 256, :] = part
        x_b16[b : b + 256, :] = part.astype(jnp.bfloat16)
    root = (1.25 * eye(start, rows) - 0.25 * x_f32[pl.ds(start, rows), :]) / jnp.sqrt(
        jnp.sqrt(scale)
    )
    pump(2)

    def quadratic(b):
        square = dot(x_b16[pl.ds(b, 256), :], x_b16[...])
        return 0.0625 * square - 0.625 * x_f32[pl.ds(b, 256), :]

    for turn in range(2):

        @pl.loop(0, order, step=256)
        def _(b):
            e = quadratic(b)
            e_f32[pl.ds(b, 256), :] = e
            e_b16[pl.ds(b, 256), :] = e.astype(jnp.bfloat16)

        pump(3 + 3 * turn)

        @pl.loop(0, order, step=256)
        def _(b):
            g = 2.0 * CENTER * e_f32[pl.ds(b, 256), :] + dot(e_b16[pl.ds(b, 256), :], e_b16[...])
            g_b16[pl.ds(b, 256), :] = g.astype(jnp.bfloat16)

        pump(4 + 3 * turn)

        @pl.loop(0, order, step=256)
        def _(b):
            x = CENTER * CENTER * x_f32[pl.ds(b, 256), :] + dot(
                x_b16[pl.ds(b, 256), :], g_b16[...]
            )
            x_f32[pl.ds(b, 256), :] = x
            x_b16[pl.ds(b, 256), :] = x.astype(jnp.bfloat16)

        root = 1.25 * root - 0.25 * dot(root.astype(jnp.bfloat16), x_b16[...])
        pump(5 + 3 * turn)

    for d in range(1, chips - 1):
        pass_on(d)

    @pl.loop(0, order, step=256)
    def _(b):
        e_b16[pl.ds(b, 256), :] = quadratic(b).astype(jnp.bfloat16)

    last = dot(root.astype(jnp.bfloat16), x_b16[...])
    for _ in range(2):
        last = CENTER * last + dot(last.astype(jnp.bfloat16), e_b16[...])
    precond = (1.25 * root - 0.25 * last).astype(jnp.bfloat16)
    pump(9)
    pass_on(chips - 1)

    for k, (i, j) in enumerate(mean_tiles):
        mean[i * rows : (i + 1) * rows, j * LANES : (j + 1) * LANES] = (
            tot[mean_place(k)] / (shards * n_rep)
        ).astype(jnp.bfloat16)
    update_ref[0] = dot(precond, mean[...]).astype(jnp.bfloat16)

    rows_copy(0).wait_recv()
    for d in range(1, chips):
        pass_copy(d).wait_recv()

    for j in range(capacity):

        def find(block, found):
            has, at = found
            here = ((owner_ref[block] == pre) & (slot_of(block) == j)).astype(jnp.int32)
            return has + here, at + here * block

        has, at = lax.fori_loop(0, n_pre, find, (jnp.int32(0), jnp.int32(0)))
        taken = jnp.full((rows, order), has, jnp.int32) > 0
        new_state_ref[0, j] = jnp.where(taken, rows_in[at], state_ref[0, j])

    for d in range(chips):
        core_copy(d).wait_send()
        rows_copy(d).wait_send()
        if d:
            route_copy(d).wait_send()
            pass_copy(d).wait_send()

    @pl.loop(0, total)
    def _(k):
        in_copy(k).wait_send()

        @pl.when(not_end)
        def _():
            out_copy(k).wait_send()


def body(n_pre, n_rep, grads, owner, state):
    order = grads.shape[2]
    rows = state.shape[2]
    blocks = order // LANES
    total = n_rep * blocks + sum(blocks - i * rows // LANES for i in range(n_rep))
    f32, b16 = jnp.float32, jnp.bfloat16
    dma = pltpu.SemaphoreType.DMA
    vmem = pl.BlockSpec(memory_space=pltpu.VMEM)
    return pl.pallas_call(
        functools.partial(kernel, n_pre, n_rep),
        out_shape=(
            jax.ShapeDtypeStruct(state.shape, f32),
            jax.ShapeDtypeStruct((1, rows, order), b16),
        ),
        in_specs=[pl.BlockSpec(memory_space=pltpu.SMEM), vmem, vmem],
        out_specs=(vmem, vmem),
        scratch_shapes=[pltpu.VMEM((total, rows, LANES), f32)] * 4
        + [pltpu.VMEM((n_pre // 2, rows, order), f32)] * 4
        + [pltpu.VMEM((n_pre, rows, order), f32)]
        + [pltpu.VMEM((order, order), t) for t in (f32, b16, f32, b16, f32, b16, b16)]
        + [dma((total,))] * 4
        + [dma((n_pre // 2,))] * 8,
        compiler_params=pltpu.CompilerParams(
            collective_id=0, has_side_effects=True, vmem_limit_bytes=40 * 1024 * 1024
        ),
        cost_estimate=pl.CostEstimate(
            flops=20 * order**3, bytes_accessed=4 * order * order * 4, transcendentals=0
        ),
    )(owner, grads, state)


def solution(mesh):
    placed = (P("rep", "pre", None, None), P(), P("pre", None, "rep", None))
    return jax.shard_map(
        functools.partial(body, mesh.shape["pre"], mesh.shape["rep"]),
        mesh=mesh,
        in_specs=placed,
        out_specs=(P("pre", None, "rep", None), P("pre", "rep", None)),
        check_vma=False,
    )
```

```python
import functools

import jax
import jax.numpy as jnp
from jax import lax
from jax.experimental import pallas as pl
from jax.experimental.pallas import tpu as pltpu
from jax.sharding import PartitionSpec as P

DAMP = 0.05
LANES = 128
LAG = 3
CENTER = 1.5625


def nt_dot(a, b):
    return lax.dot_general(a, b, (((1,), (1,)), ((), ())), preferred_element_type=jnp.float32)


def dot(a, b):
    return jnp.dot(a, b, preferred_element_type=jnp.float32)


def kernel(
    n_pre,
    n_rep,
    owner_ref,
    grads_hbm,
    state_hbm,
    new_state_ref,
    update_ref,
    grads_ref,
    state_ref,
    loc,
    up,
    dn,
    tot,
    core_out,
    core_in,
    route_out,
    route_in,
    rows_in,
    stat,
    mean,
    x_f32,
    x_b16,
    e_f32,
    e_b16,
    g_b16,
    in_send,
    out_send,
    up_recv,
    dn_recv,
    core_send,
    core_recv,
    route_send,
    route_recv,
    rows_send,
    rows_recv,
    pass_send,
    pass_recv,
    load_sem,
):
    pre, rep = lax.axis_index("pre"), lax.axis_index("rep")
    shards, order = grads_ref.shape[0], grads_ref.shape[2]
    rows = state_ref.shape[2]
    blocks = order // LANES
    half = n_rep // 2
    is_end = (rep == 0) | (rep == n_rep - 1)
    is_mid = (rep == half - 1) | (rep == half)
    not_end, not_mid = jnp.logical_not(is_end), jnp.logical_not(is_mid)
    inward = jnp.where(rep < half, rep + 1, rep - 1)
    outward = jnp.where(rep < half, rep - 1, rep + 1)
    chips, chip, core = n_pre // 2, pre // 2, pre % 2
    partner = pre + 1 - 2 * core

    def chip_at(d):
        other, bit = chip, 1
        while bit < chips:
            if d & bit:
                other = other + bit * (1 - 2 * ((chip // bit) % 2))
            bit *= 2
        return other

    mean_tiles = [(i, j) for i in range(n_rep) for j in range(blocks)]
    bands_out = sorted(range(n_rep), key=lambda i: abs(2 * i + 1 - n_rep))
    stat_tiles = [(i, j) for i in bands_out for j in range(i * rows // LANES, blocks)]
    free = sum(0 < i < n_rep - 1 for i, _ in stat_tiles)
    early = len(mean_tiles) // 2
    after = early + len(stat_tiles)
    total = len(mean_tiles) + len(stat_tiles)

    def mean_place(k):
        return k if k < early else k + len(stat_tiles)

    def remote(src, dst, send, recv, device):
        return pltpu.make_async_remote_copy(
            src_ref=src,
            dst_ref=dst,
            send_sem=send,
            recv_sem=recv,
            device_id=device,
            device_id_type=pl.DeviceIdType.MESH,
        )

    def load(a):
        band = slice(a * LANES, (a + 1) * LANES)
        return pltpu.make_async_copy(
            grads_hbm.at[:, :, band, :], grads_ref.at[:, :, band, :], load_sem.at[a]
        )

    load_state = pltpu.make_async_copy(state_hbm, state_ref, load_sem.at[blocks])
    load_state.start()
    for a in range(blocks):
        load(a).start()

    count = first = second = jnp.int32(0)
    for b in range(n_pre):
        here = owner_ref[b] == pre
        first = jnp.where(here & (count == 0), b, first)
        second = jnp.where(here & (count == 1), b, second)
        count = count + here.astype(jnp.int32)

    barrier = pltpu.get_barrier_semaphore()

    def greet(device):
        pl.semaphore_signal(
            barrier, inc=1, device_id=device, device_id_type=pl.DeviceIdType.MESH
        )

    for d in range(1, chips):
        greet({"pre": 2 * chip_at(d) + core})
    greet({"pre": partner})
    greet({"rep": inward})

    @pl.when(not_end)
    def _():
        greet({"rep": outward})

    pl.semaphore_wait(barrier, jnp.where(is_end, chips + 1, chips + 2))

    def send_in(k):
        @pl.when(is_mid)
        def _():
            remote(
                loc.at[k], dn.at[k], in_send.at[k], dn_recv.at[k], {"rep": inward}
            ).start()

        @pl.when(not_mid)
        def _():
            remote(
                loc.at[k], up.at[k], in_send.at[k], up_recv.at[k], {"rep": inward}
            ).start()

    def out_copy(k):
        return remote(tot.at[k], dn.at[k], out_send.at[k], dn_recv.at[k], {"rep": outward})

    def in_copy(k):
        return remote(loc.at[k], up.at[k], in_send.at[k], up_recv.at[k], {"rep": inward})

    def step_up(k):
        @pl.when(not_end)
        def _():
            in_copy(k).wait_recv()
            loc[k] = loc[k] + up[k]
            send_in(k)

    def step_down(k):
        out_copy(k).wait_recv()

        @pl.when(is_mid)
        def _():
            tot[k] = loc[k] + dn[k]

        @pl.when(not_mid)
        def _():
            tot[k] = dn[k]

        @pl.when(not_end)
        def _():
            out_copy(k).start()

    def piece(block):
        return state_ref[0, ((count > 1) & (second == block)).astype(jnp.int32)]

    def core_copy(d):
        return remote(
            core_out.at[d], core_in.at[d], core_send.at[d], core_recv.at[d], {"pre": partner}
        )

    def route_copy(d):
        return remote(
            route_out.at[d],
            route_in.at[chip],
            route_send.at[d],
            route_recv.at[d],
            {"pre": 2 * chip_at(d) + core},
        )

    load_state.wait()
    far_first = list(range(chips - 1, -1, -1))
    for d in far_first:
        core_out[d] = piece(2 * chip_at(d) + 1 - core)
        core_copy(d).start()

    for k, (i, j) in enumerate(mean_tiles):
        if j == 0 and i * rows % LANES == 0:
            load(i * rows // LANES).wait()
        r, c = slice(i * rows, (i + 1) * rows), slice(j * LANES, (j + 1) * LANES)
        acc = grads_ref[0, 0, r, c].astype(jnp.float32)
        for s in range(1, shards):
            acc = acc + grads_ref[s, 0, r, c].astype(jnp.float32)
        loc[mean_place(k)] = acc
        if k < early:

            @pl.when(is_end)
            def _():
                send_in(k)

    for d in far_first:
        block = 2 * chip_at(d) + core
        core_copy(d).wait_recv()
        theirs = jnp.full((rows, order), (owner_ref[block] == partner).astype(jnp.int32)) > 0
        chosen = jnp.where(theirs, core_in[d], piece(block))
        if d:
            route_out[d] = chosen
            route_copy(d).start()
        else:
            route_in[chip] = chosen

    for a in range(blocks):
        low = a * LANES
        gram = nt_dot(grads_ref[0, 0, low : low + LANES, :], grads_ref[0, 0, low:, :])
        for s in range(1, shards):
            gram = gram + nt_dot(grads_ref[s, 0, low : low + LANES, :], grads_ref[s, 0, low:, :])
        for k, (i, j) in enumerate(stat_tiles):
            if i * rows // LANES == a:
                r = i * rows - low
                loc[early + k] = gram[r : r + rows, j * LANES - low : (j + 1) * LANES - low]

    def inject():
        for d in range(1, chips):
            route_copy(d).wait_recv()
        held = route_in[owner_ref[pre] // 2]
        for k, (i, j) in enumerate(stat_tiles):

            @pl.when(rep == i)
            def _():
                loc[early + k] = loc[early + k] + held[:, j * LANES : (j + 1) * LANES]

    @pl.when(is_end)
    def _():
        @pl.loop(early, early + free)
        def _(k):
            send_in(k)

        inject()

        @pl.loop(early + free, total)
        def _(k):
            send_in(k)

    @pl.loop(0, LAG)
    def _(k):
        step_up(k)

    @pl.loop(LAG, early)
    def _(k):
        step_up(k)
        step_down(k - LAG)

    @pl.when(not_end)
    def _():
        inject()

    @pl.loop(early, after + LAG)
    def _(k):
        step_up(k)
        step_down(k - LAG)

    def pump(part, parts=10):
        left = total - after
        for k in range(left * part // parts, left * (part + 1) // parts):

            @pl.when(not_end)
            def _():
                if after + LAG + k < total:
                    step_up(after + LAG + k)
                step_down(after + k)

    for k, (i, j) in enumerate(stat_tiles):
        stat[i * rows : (i + 1) * rows, j * LANES : (j + 1) * LANES] = tot[early + k]
    for a in range(blocks):
        for b in range(a + 1, blocks):
            ra, rb = slice(a * LANES, (a + 1) * LANES), slice(b * LANES, (b + 1) * LANES)
            stat[rb, ra] = stat[ra, rb].T

    start = pl.multiple_of(rep * rows, rows)

    def rows_copy(d):
        device = {"pre": 2 * chip_at(d) + core} if d else {"pre": partner}
        return remote(
            stat.at[pl.ds(start, rows)],
            rows_in.at[pre],
            rows_send.at[d],
            rows_recv.at[d],
            device,
        )

    def pass_copy(d):
        held = rows_in.at[2 * chip_at(d) + core]
        return remote(held, held, pass_send.at[d], pass_recv.at[d], {"pre": partner})

    def pass_on(d):
        rows_copy(d).wait_recv()
        pass_copy(d).start()

    for d in range(1, chips):
        rows_copy(d).start()
    rows_copy(0).start()
    rows_in[pre] = stat[pl.ds(start, rows), :]
    pump(0)

    def eye(first, count):
        r = lax.broadcasted_iota(jnp.int32, (count, order), 0) + first
        c = lax.broadcasted_iota(jnp.int32, (count, order), 1)
        return (r == c).astype(jnp.float32)

    bands = range(0, order, 256)
    squares = jnp.zeros((1, 1), jnp.float32)
    for b in bands:
        part = stat[b : b + 256, :]
        squares = squares + jnp.sum(part * part, keepdims=True)
    shift = DAMP * jnp.sqrt(squares)
    squares = jnp.zeros((1, 1), jnp.float32)
    for b in bands:
        part = stat[b : b + 256, :] + shift * eye(b, 256)
        x_f32[b : b + 256, :] = part
        squares = squares + jnp.sum(part * part, keepdims=True)
    scale = jnp.sqrt(squares)
    pump(1)
    for b in bands:
        part = x_f32[b : b + 256, :] / scale
        x_f32[b : b + 256, :] = part
        x_b16[b : b + 256, :] = part.astype(jnp.bfloat16)
    root = (1.25 * eye(start, rows) - 0.25 * x_f32[pl.ds(start, rows), :]) / jnp.sqrt(
        jnp.sqrt(scale)
    )
    pump(2)

    def quadratic(b):
        square = dot(x_b16[pl.ds(b, 256), :], x_b16[...])
        return 0.0625 * square - 0.625 * x_f32[pl.ds(b, 256), :]

    for turn in range(2):

        @pl.loop(0, order, step=256)
        def _(b):
            e = quadratic(b)
            e_f32[pl.ds(b, 256), :] = e
            e_b16[pl.ds(b, 256), :] = e.astype(jnp.bfloat16)

        pump(3 + 3 * turn)

        @pl.loop(0, order, step=256)
        def _(b):
            g = 2.0 * CENTER * e_f32[pl.ds(b, 256), :] + dot(e_b16[pl.ds(b, 256), :], e_b16[...])
            g_b16[pl.ds(b, 256), :] = g.astype(jnp.bfloat16)

        pump(4 + 3 * turn)

        @pl.loop(0, order, step=256)
        def _(b):
            x = CENTER * CENTER * x_f32[pl.ds(b, 256), :] + dot(
                x_b16[pl.ds(b, 256), :], g_b16[...]
            )
            x_f32[pl.ds(b, 256), :] = x
            x_b16[pl.ds(b, 256), :] = x.astype(jnp.bfloat16)

        root = 1.25 * root - 0.25 * dot(root.astype(jnp.bfloat16), x_b16[...])
        pump(5 + 3 * turn)

    for d in range(1, chips - 1):
        pass_on(d)

    @pl.loop(0, order, step=256)
    def _(b):
        e_b16[pl.ds(b, 256), :] = quadratic(b).astype(jnp.bfloat16)

    last = dot(root.astype(jnp.bfloat16), x_b16[...])
    for _ in range(2):
        last = CENTER * last + dot(last.astype(jnp.bfloat16), e_b16[...])
    precond = (1.25 * root - 0.25 * last).astype(jnp.bfloat16)
    pump(9)
    pass_on(chips - 1)

    @pl.when(is_end)
    def _():
        @pl.loop(after, total)
        def _(k):
            step_down(k)

    for k, (i, j) in enumerate(mean_tiles):
        mean[i * rows : (i + 1) * rows, j * LANES : (j + 1) * LANES] = (
            tot[mean_place(k)] / (shards * n_rep)
        ).astype(jnp.bfloat16)
    update_ref[0] = dot(precond, mean[...]).astype(jnp.bfloat16)

    rows_copy(0).wait_recv()
    for d in range(1, chips):
        pass_copy(d).wait_recv()

    for j, at in enumerate((first, second)):
        taken = jnp.full((rows, order), count, jnp.int32) > j
        new_state_ref[0, j] = jnp.where(taken, rows_in[at], state_ref[0, j])

    for d in range(chips):
        core_copy(d).wait_send()
        rows_copy(d).wait_send()
        if d:
            route_copy(d).wait_send()
            pass_copy(d).wait_send()

    @pl.loop(0, total)
    def _(k):
        in_copy(k).wait_send()

        @pl.when(not_end)
        def _():
            out_copy(k).wait_send()


def body(n_pre, n_rep, grads, owner, state):
    order = grads.shape[2]
    rows = state.shape[2]
    blocks = order // LANES
    total = n_rep * blocks + sum(blocks - i * rows // LANES for i in range(n_rep))
    f32, b16 = jnp.float32, jnp.bfloat16
    dma = pltpu.SemaphoreType.DMA
    vmem = pl.BlockSpec(memory_space=pltpu.VMEM)
    return pl.pallas_call(
        functools.partial(kernel, n_pre, n_rep),
        out_shape=(
            jax.ShapeDtypeStruct(state.shape, f32),
            jax.ShapeDtypeStruct((1, rows, order), b16),
        ),
        in_specs=[pl.BlockSpec(memory_space=pltpu.SMEM)]
        + [pl.BlockSpec(memory_space=pltpu.HBM)] * 2,
        out_specs=(vmem, vmem),
        scratch_shapes=[pltpu.VMEM(grads.shape, b16), pltpu.VMEM(state.shape, f32)]
        + [pltpu.VMEM((total, rows, LANES), f32)] * 4
        + [pltpu.VMEM((n_pre // 2, rows, order), f32)] * 4
        + [pltpu.VMEM((n_pre, rows, order), f32)]
        + [pltpu.VMEM((order, order), t) for t in (f32, b16, f32, b16, f32, b16, b16)]
        + [dma((total,))] * 4
        + [dma((n_pre // 2,))] * 8
        + [dma((blocks + 1,))],
        compiler_params=pltpu.CompilerParams(
            collective_id=0, has_side_effects=True, vmem_limit_bytes=40 * 1024 * 1024
        ),
        cost_estimate=pl.CostEstimate(
            flops=20 * order**3, bytes_accessed=4 * order * order * 4, transcendentals=0
        ),
    )(owner, grads, state)


def solution(mesh):
    placed = (P("rep", "pre", None, None), P(), P("pre", None, "rep", None))
    return jax.shard_map(
        functools.partial(body, mesh.shape["pre"], mesh.shape["rep"]),
        mesh=mesh,
        in_specs=placed,
        out_specs=(P("pre", None, "rep", None), P("pre", "rep", None)),
        check_vma=False,
    )
```

```python
import functools

import jax
import jax.numpy as jnp
from jax import lax
from jax.experimental import pallas as pl
from jax.experimental.pallas import tpu as pltpu
from jax.sharding import PartitionSpec as P

DAMP = 0.05
LANES = 128
LAG = 3
CENTER = 1.5625


def nt_dot(a, b):
    return lax.dot_general(a, b, (((1,), (1,)), ((), ())), preferred_element_type=jnp.float32)


def dot(a, b):
    return jnp.dot(a, b, preferred_element_type=jnp.float32)


def kernel(
    n_pre,
    n_rep,
    owner_ref,
    grads_hbm,
    state_hbm,
    new_state_ref,
    update_ref,
    grads_ref,
    state_ref,
    loc,
    up,
    dn,
    tot,
    core_out,
    core_in,
    route_out,
    route_in,
    rows_in,
    stat,
    mean,
    x_f32,
    x_b16,
    e_f32,
    e_b16,
    g_b16,
    in_send,
    out_send,
    up_recv,
    dn_recv,
    core_send,
    core_recv,
    route_send,
    route_recv,
    rows_send,
    rows_recv,
    pass_send,
    pass_recv,
    load_sem,
):
    pre, rep = lax.axis_index("pre"), lax.axis_index("rep")
    shards, order = grads_ref.shape[0], grads_ref.shape[2]
    rows = state_ref.shape[2]
    blocks = order // LANES
    half = n_rep // 2
    is_end = (rep == 0) | (rep == n_rep - 1)
    is_mid = (rep == half - 1) | (rep == half)
    not_end, not_mid = jnp.logical_not(is_end), jnp.logical_not(is_mid)
    inward = jnp.where(rep < half, rep + 1, rep - 1)
    outward = jnp.where(rep < half, rep - 1, rep + 1)
    chips, chip, core = n_pre // 2, pre // 2, pre % 2
    partner = pre + 1 - 2 * core

    def chip_at(d):
        other, bit = chip, 1
        while bit < chips:
            if d & bit:
                other = other + bit * (1 - 2 * ((chip // bit) % 2))
            bit *= 2
        return other

    mean_tiles = [(i, j) for i in range(n_rep) for j in range(blocks)]
    bands_out = sorted(range(n_rep), key=lambda i: abs(2 * i + 1 - n_rep))
    stat_tiles = [(i, j) for i in bands_out for j in range(i * rows // LANES, blocks)]
    free = sum(0 < i < n_rep - 1 for i, _ in stat_tiles)
    early = len(mean_tiles) * 3 // 8
    after = early + len(stat_tiles)
    total = len(mean_tiles) + len(stat_tiles)

    def mean_place(k):
        return k if k < early else k + len(stat_tiles)

    def remote(src, dst, send, recv, device):
        return pltpu.make_async_remote_copy(
            src_ref=src,
            dst_ref=dst,
            send_sem=send,
            recv_sem=recv,
            device_id=device,
            device_id_type=pl.DeviceIdType.MESH,
        )

    def load(a):
        band = slice(a * LANES, (a + 1) * LANES)
        return pltpu.make_async_copy(
            grads_hbm.at[:, :, band, :], grads_ref.at[:, :, band, :], load_sem.at[a]
        )

    load_state = pltpu.make_async_copy(state_hbm, state_ref, load_sem.at[blocks])
    load_state.start()
    for a in range(blocks):
        load(a).start()

    count = first = second = jnp.int32(0)
    for b in range(n_pre):
        here = owner_ref[b] == pre
        first = jnp.where(here & (count == 0), b, first)
        second = jnp.where(here & (count == 1), b, second)
        count = count + here.astype(jnp.int32)

    barrier = pltpu.get_barrier_semaphore()

    def greet(device):
        pl.semaphore_signal(
            barrier, inc=1, device_id=device, device_id_type=pl.DeviceIdType.MESH
        )

    for d in range(1, chips):
        greet({"pre": 2 * chip_at(d) + core})
    greet({"pre": partner})
    greet({"rep": inward})

    @pl.when(not_end)
    def _():
        greet({"rep": outward})

    pl.semaphore_wait(barrier, jnp.where(is_end, chips + 1, chips + 2))

    def send_in(k):
        @pl.when(is_mid)
        def _():
            remote(
                loc.at[k], dn.at[k], in_send.at[k], dn_recv.at[k], {"rep": inward}
            ).start()

        @pl.when(not_mid)
        def _():
            remote(
                loc.at[k], up.at[k], in_send.at[k], up_recv.at[k], {"rep": inward}
            ).start()

    def out_copy(k):
        return remote(tot.at[k], dn.at[k], out_send.at[k], dn_recv.at[k], {"rep": outward})

    def in_copy(k):
        return remote(loc.at[k], up.at[k], in_send.at[k], up_recv.at[k], {"rep": inward})

    def step_up(k):
        @pl.when(not_end)
        def _():
            in_copy(k).wait_recv()
            loc[k] = loc[k] + up[k]
            send_in(k)

    def step_down(k):
        out_copy(k).wait_recv()

        @pl.when(is_mid)
        def _():
            tot[k] = loc[k] + dn[k]

        @pl.when(not_mid)
        def _():
            tot[k] = dn[k]

        @pl.when(not_end)
        def _():
            out_copy(k).start()

    def piece(block, j):
        at = ((count > 1) & (second == block)).astype(jnp.int32)
        return state_ref[0, at, :, j * LANES : (j + 1) * LANES]

    def core_copy(d, j):
        return remote(
            core_out.at[d, j],
            core_in.at[d, j],
            core_send.at[d, j],
            core_recv.at[d, j],
            {"pre": partner},
        )

    def route_copy(d, j):
        return remote(
            route_out.at[d, j],
            route_in.at[chip, j],
            route_send.at[d, j],
            route_recv.at[d, j],
            {"pre": 2 * chip_at(d) + core},
        )

    def needed(j):
        return pl.when(rep * rows < (j + 1) * LANES)

    load_state.wait()
    far_first = list(range(chips - 1, -1, -1))
    columns = range(blocks - 1, -1, -1)
    for j in columns:

        @needed(j)
        def _():
            for d in far_first:
                core_out[d, j] = piece(2 * chip_at(d) + 1 - core, j)
                core_copy(d, j).start()

    for k, (i, j) in enumerate(mean_tiles):
        if j == 0 and i * rows % LANES == 0:
            load(i * rows // LANES).wait()
        r, c = slice(i * rows, (i + 1) * rows), slice(j * LANES, (j + 1) * LANES)
        acc = grads_ref[0, 0, r, c].astype(jnp.float32)
        for s in range(1, shards):
            acc = acc + grads_ref[s, 0, r, c].astype(jnp.float32)
        loc[mean_place(k)] = acc
        if k < early:

            @pl.when(is_end)
            def _():
                send_in(k)

    for j in columns:

        @needed(j)
        def _():
            for d in far_first:
                block = 2 * chip_at(d) + core
                core_copy(d, j).wait_recv()
                theirs = (owner_ref[block] == partner).astype(jnp.int32)
                chosen = jnp.where(
                    jnp.full((rows, LANES), theirs) > 0, core_in[d, j], piece(block, j)
                )
                if d:
                    route_out[d, j] = chosen
                    route_copy(d, j).start()
                else:
                    route_in[chip, j] = chosen

    for a in range(blocks):
        low = a * LANES
        gram = nt_dot(grads_ref[0, 0, low : low + LANES, :], grads_ref[0, 0, low:, :])
        for s in range(1, shards):
            gram = gram + nt_dot(grads_ref[s, 0, low : low + LANES, :], grads_ref[s, 0, low:, :])
        for k, (i, j) in enumerate(stat_tiles):
            if i * rows // LANES == a:
                r = i * rows - low
                loc[early + k] = gram[r : r + rows, j * LANES - low : (j + 1) * LANES - low]

    def inject():
        for j in range(blocks):

            @needed(j)
            def _():
                for d in range(1, chips):
                    route_copy(d, j).wait_recv()

        for k, (i, j) in enumerate(stat_tiles):

            @pl.when(rep == i)
            def _():
                loc[early + k] = loc[early + k] + route_in[owner_ref[pre] // 2, j]

    @pl.when(is_end)
    def _():
        @pl.loop(early, early + free)
        def _(k):
            send_in(k)

        inject()

        @pl.loop(early + free, total)
        def _(k):
            send_in(k)

    @pl.loop(0, LAG)
    def _(k):
        step_up(k)

    @pl.loop(LAG, early)
    def _(k):
        step_up(k)
        step_down(k - LAG)

    @pl.when(not_end)
    def _():
        inject()

    start = pl.multiple_of(rep * rows, rows)

    def rows_copy(d, j):
        device = {"pre": 2 * chip_at(d) + core} if d else {"pre": partner}
        return remote(
            stat.at[pl.ds(start, rows), pl.ds(j * LANES, LANES)],
            rows_in.at[pre, j],
            rows_send.at[d, j],
            rows_recv.at[d, j],
            device,
        )

    def pass_copy(d, j):
        held = rows_in.at[2 * chip_at(d) + core, j]
        return remote(held, held, pass_send.at[d, j], pass_recv.at[d, j], {"pre": partner})

    def pass_on(d, j):
        rows_copy(d, j).wait_recv()
        pass_copy(d, j).start()

    def send_rows(j):
        for d in far_first:
            rows_copy(d, j).start()

    @pl.loop(early, early + LAG)
    def _(k):
        step_up(k)
        step_down(k - LAG)

    for k, (i, j) in enumerate(stat_tiles):
        step_up(early + LAG + k)
        step_down(early + k)
        rs, cs = slice(i * rows, (i + 1) * rows), slice(j * LANES, (j + 1) * LANES)
        stat[rs, cs] = tot[early + k]
        if rows == LANES:

            @pl.when(rep == i)
            def _():
                send_rows(j)

            if i != j:
                stat[cs, rs] = tot[early + k].T

                @pl.when(rep == j)
                def _():
                    send_rows(i)

    if rows != LANES:
        for a in range(blocks):
            for b in range(a + 1, blocks):
                ra, rb = slice(a * LANES, (a + 1) * LANES), slice(b * LANES, (b + 1) * LANES)
                stat[rb, ra] = stat[ra, rb].T
        for j in range(blocks):
            send_rows(j)
    for j in range(blocks):
        rows_in[pre, j] = stat[pl.ds(start, rows), j * LANES : (j + 1) * LANES]

    def pump(part, parts=10):
        left = total - after
        for k in range(left * part // parts, left * (part + 1) // parts):

            @pl.when(not_end)
            def _():
                if after + LAG + k < total:
                    step_up(after + LAG + k)
                step_down(after + k)

    pump(0)

    def eye(first, count):
        r = lax.broadcasted_iota(jnp.int32, (count, order), 0) + first
        c = lax.broadcasted_iota(jnp.int32, (count, order), 1)
        return (r == c).astype(jnp.float32)

    bands = range(0, order, 256)
    squares = jnp.zeros((1, 1), jnp.float32)
    for b in bands:
        part = stat[b : b + 256, :]
        squares = squares + jnp.sum(part * part, keepdims=True)
    shift = DAMP * jnp.sqrt(squares)
    squares = jnp.zeros((1, 1), jnp.float32)
    for b in bands:
        part = stat[b : b + 256, :] + shift * eye(b, 256)
        x_f32[b : b + 256, :] = part
        squares = squares + jnp.sum(part * part, keepdims=True)
    scale = jnp.sqrt(squares)
    pump(1)
    for b in bands:
        part = x_f32[b : b + 256, :] / scale
        x_f32[b : b + 256, :] = part
        x_b16[b : b + 256, :] = part.astype(jnp.bfloat16)
    root = (1.25 * eye(start, rows) - 0.25 * x_f32[pl.ds(start, rows), :]) / jnp.sqrt(
        jnp.sqrt(scale)
    )
    pump(2)

    def quadratic(b):
        square = dot(x_b16[pl.ds(b, 256), :], x_b16[...])
        return 0.0625 * square - 0.625 * x_f32[pl.ds(b, 256), :]

    for turn in range(2):

        @pl.loop(0, order, step=256)
        def _(b):
            e = quadratic(b)
            e_f32[pl.ds(b, 256), :] = e
            e_b16[pl.ds(b, 256), :] = e.astype(jnp.bfloat16)

        pump(3 + 3 * turn)

        @pl.loop(0, order, step=256)
        def _(b):
            g = 2.0 * CENTER * e_f32[pl.ds(b, 256), :] + dot(e_b16[pl.ds(b, 256), :], e_b16[...])
            g_b16[pl.ds(b, 256), :] = g.astype(jnp.bfloat16)

        pump(4 + 3 * turn)

        @pl.loop(0, order, step=256)
        def _(b):
            x = CENTER * CENTER * x_f32[pl.ds(b, 256), :] + dot(
                x_b16[pl.ds(b, 256), :], g_b16[...]
            )
            x_f32[pl.ds(b, 256), :] = x
            x_b16[pl.ds(b, 256), :] = x.astype(jnp.bfloat16)

        root = 1.25 * root - 0.25 * dot(root.astype(jnp.bfloat16), x_b16[...])
        pump(5 + 3 * turn)

    for d in range(1, chips - 1):
        for j in range(blocks):
            pass_on(d, j)

    @pl.loop(0, order, step=256)
    def _(b):
        e_b16[pl.ds(b, 256), :] = quadratic(b).astype(jnp.bfloat16)

    last = dot(root.astype(jnp.bfloat16), x_b16[...])
    for _ in range(2):
        last = CENTER * last + dot(last.astype(jnp.bfloat16), e_b16[...])
    precond = (1.25 * root - 0.25 * last).astype(jnp.bfloat16)
    pump(9)
    for j in range(blocks):
        pass_on(chips - 1, j)

    @pl.when(is_end)
    def _():
        @pl.loop(after, total)
        def _(k):
            step_down(k)

    for k, (i, j) in enumerate(mean_tiles):
        mean[i * rows : (i + 1) * rows, j * LANES : (j + 1) * LANES] = (
            tot[mean_place(k)] / (shards * n_rep)
        ).astype(jnp.bfloat16)
    update_ref[0] = dot(precond, mean[...]).astype(jnp.bfloat16)

    for j in range(blocks):
        rows_copy(0, j).wait_recv()
        for d in range(1, chips):
            pass_copy(d, j).wait_recv()
    for j in range(blocks):
        cs = slice(j * LANES, (j + 1) * LANES)
        for held, at in enumerate((first, second)):
            taken = jnp.full((rows, LANES), count, jnp.int32) > held
            new_state_ref[0, held, :, cs] = jnp.where(
                taken, rows_in[at, j], state_ref[0, held, :, cs]
            )

    for j in range(blocks):

        @needed(j)
        def _():
            for d in range(chips):
                core_copy(d, j).wait_send()
                if d:
                    route_copy(d, j).wait_send()

        for d in range(chips):
            rows_copy(d, j).wait_send()
            if d:
                pass_copy(d, j).wait_send()

    @pl.loop(0, total)
    def _(k):
        in_copy(k).wait_send()

        @pl.when(not_end)
        def _():
            out_copy(k).wait_send()


def body(n_pre, n_rep, grads, owner, state):
    order = grads.shape[2]
    rows = state.shape[2]
    blocks = order // LANES
    total = n_rep * blocks + sum(blocks - i * rows // LANES for i in range(n_rep))
    f32, b16 = jnp.float32, jnp.bfloat16
    dma = pltpu.SemaphoreType.DMA
    vmem = pl.BlockSpec(memory_space=pltpu.VMEM)
    return pl.pallas_call(
        functools.partial(kernel, n_pre, n_rep),
        out_shape=(
            jax.ShapeDtypeStruct(state.shape, f32),
            jax.ShapeDtypeStruct((1, rows, order), b16),
        ),
        in_specs=[pl.BlockSpec(memory_space=pltpu.SMEM)]
        + [pl.BlockSpec(memory_space=pltpu.HBM)] * 2,
        out_specs=(vmem, vmem),
        scratch_shapes=[pltpu.VMEM(grads.shape, b16), pltpu.VMEM(state.shape, f32)]
        + [pltpu.VMEM((total, rows, LANES), f32)] * 4
        + [pltpu.VMEM((n_pre // 2, blocks, rows, LANES), f32)] * 4
        + [pltpu.VMEM((n_pre, blocks, rows, LANES), f32)]
        + [pltpu.VMEM((order, order), t) for t in (f32, b16, f32, b16, f32, b16, b16)]
        + [dma((total,))] * 4
        + [dma((n_pre // 2, blocks))] * 8
        + [dma((blocks + 1,))],
        compiler_params=pltpu.CompilerParams(
            collective_id=0, has_side_effects=True, vmem_limit_bytes=60 * 1024 * 1024
        ),
        cost_estimate=pl.CostEstimate(
            flops=20 * order**3, bytes_accessed=4 * order * order * 4, transcendentals=0
        ),
    )(owner, grads, state)


def solution(mesh):
    placed = (P("rep", "pre", None, None), P(), P("pre", None, "rep", None))
    return jax.shard_map(
        functools.partial(body, mesh.shape["pre"], mesh.shape["rep"]),
        mesh=mesh,
        in_specs=placed,
        out_specs=(P("pre", None, "rep", None), P("pre", "rep", None)),
        check_vma=False,
    )
```

```python
import functools

import jax
import jax.numpy as jnp
from jax import lax
from jax.experimental import pallas as pl
from jax.experimental.pallas import tpu as pltpu
from jax.sharding import PartitionSpec as P

DAMP = 0.05
LANES = 128
LAG = 2
CENTER = 1.5625


def nt_dot(a, b):
    return lax.dot_general(a, b, (((1,), (1,)), ((), ())), preferred_element_type=jnp.float32)


def dot(a, b):
    return jnp.dot(a, b, preferred_element_type=jnp.float32)


def kernel(
    n_pre,
    n_rep,
    owner_ref,
    grads_hbm,
    state_hbm,
    gain_ref,
    update_ref,
    grads_ref,
    state_ref,
    loc,
    up,
    dn,
    tot,
    core_out,
    core_in,
    route_out,
    route_in,
    rows_in,
    stat,
    mean,
    x_f32,
    x_b16,
    e_f32,
    e_b16,
    g_b16,
    in_send,
    out_send,
    up_recv,
    dn_recv,
    core_send,
    core_recv,
    route_send,
    route_recv,
    rows_send,
    rows_recv,
    pass_send,
    pass_recv,
    load_sem,
):
    pre, rep = lax.axis_index("pre"), lax.axis_index("rep")
    shards, order = grads_ref.shape[0], grads_ref.shape[2]
    rows = state_ref.shape[2]
    blocks = order // LANES
    half = n_rep // 2
    is_end = (rep == 0) | (rep == n_rep - 1)
    is_mid = (rep == half - 1) | (rep == half)
    not_end, not_mid = jnp.logical_not(is_end), jnp.logical_not(is_mid)
    inward = jnp.where(rep < half, rep + 1, rep - 1)
    outward = jnp.where(rep < half, rep - 1, rep + 1)
    chips, chip, core = n_pre // 2, pre // 2, pre % 2
    partner = pre + 1 - 2 * core

    def chip_at(d):
        other, bit = chip, 1
        while bit < chips:
            if d & bit:
                other = other + bit * (1 - 2 * ((chip // bit) % 2))
            bit *= 2
        return other

    mean_tiles = [(i, j) for i in range(n_rep) for j in range(blocks)]
    bands_out = sorted(range(n_rep), key=lambda i: abs(2 * i + 1 - n_rep))
    stat_tiles = [(i, j) for i in bands_out for j in range(i * rows // LANES, blocks)]
    free = sum(0 < i < n_rep - 1 for i, _ in stat_tiles)
    early = len(mean_tiles) * 3 // 8
    after = early + len(stat_tiles)
    total = len(mean_tiles) + len(stat_tiles)

    def mean_place(k):
        return k if k < early else k + len(stat_tiles)

    def remote(src, dst, send, recv, device):
        return pltpu.make_async_remote_copy(
            src_ref=src,
            dst_ref=dst,
            send_sem=send,
            recv_sem=recv,
            device_id=device,
            device_id_type=pl.DeviceIdType.MESH,
        )

    def load(a):
        band = slice(a * LANES, (a + 1) * LANES)
        return pltpu.make_async_copy(
            grads_hbm.at[:, :, band, :], grads_ref.at[:, :, band, :], load_sem.at[a]
        )

    load_state = pltpu.make_async_copy(state_hbm, state_ref, load_sem.at[blocks])
    load_state.start()
    for a in range(blocks):
        load(a).start()

    count = first = second = jnp.int32(0)
    for b in range(n_pre):
        here = owner_ref[b] == pre
        first = jnp.where(here & (count == 0), b, first)
        second = jnp.where(here & (count == 1), b, second)
        count = count + here.astype(jnp.int32)

    barrier = pltpu.get_barrier_semaphore()

    def greet(device):
        pl.semaphore_signal(
            barrier, inc=1, device_id=device, device_id_type=pl.DeviceIdType.MESH
        )

    for d in range(1, chips):
        greet({"pre": 2 * chip_at(d) + core})
    greet({"pre": partner})
    greet({"rep": inward})

    @pl.when(not_end)
    def _():
        greet({"rep": outward})

    pl.semaphore_wait(barrier, jnp.where(is_end, chips + 1, chips + 2))

    def send_in(k):
        @pl.when(is_mid)
        def _():
            remote(
                loc.at[k], dn.at[k], in_send.at[k], dn_recv.at[k], {"rep": inward}
            ).start()

        @pl.when(not_mid)
        def _():
            remote(
                loc.at[k], up.at[k], in_send.at[k], up_recv.at[k], {"rep": inward}
            ).start()

    def out_copy(k):
        return remote(tot.at[k], dn.at[k], out_send.at[k], dn_recv.at[k], {"rep": outward})

    def in_copy(k):
        return remote(loc.at[k], up.at[k], in_send.at[k], up_recv.at[k], {"rep": inward})

    def step_up(k):
        @pl.when(not_end)
        def _():
            in_copy(k).wait_recv()
            loc[k] = loc[k] + up[k]
            send_in(k)

    def step_down(k):
        out_copy(k).wait_recv()

        @pl.when(is_mid)
        def _():
            tot[k] = loc[k] + dn[k]

        @pl.when(not_mid)
        def _():
            tot[k] = dn[k]

        @pl.when(not_end)
        def _():
            out_copy(k).start()

    def add_shards(k):
        i, j = mean_tiles[k]
        if j == 0 and i * rows % LANES == 0:
            load(i * rows // LANES).wait()
        r, c = slice(i * rows, (i + 1) * rows), slice(j * LANES, (j + 1) * LANES)
        acc = grads_ref[0, 0, r, c].astype(jnp.float32)
        for s in range(1, shards):
            acc = acc + grads_ref[s, 0, r, c].astype(jnp.float32)
        loc[mean_place(k)] = acc
        if k < early:

            @pl.when(is_end)
            def _():
                send_in(k)

    for k in range(blocks):
        add_shards(k)

    def piece(block, j):
        at = ((count > 1) & (second == block)).astype(jnp.int32)
        return state_ref[0, at, :, j * LANES : (j + 1) * LANES]

    def core_copy(d, j):
        return remote(
            core_out.at[d, j],
            core_in.at[d, j],
            core_send.at[d, j],
            core_recv.at[d, j],
            {"pre": partner},
        )

    def route_copy(d, j):
        return remote(
            route_out.at[d, j],
            route_in.at[chip, j],
            route_send.at[d, j],
            route_recv.at[d, j],
            {"pre": 2 * chip_at(d) + core},
        )

    def needed(j):
        return pl.when(rep * rows < (j + 1) * LANES)

    load_state.wait()
    far_first = list(range(chips - 1, -1, -1))
    columns = range(blocks - 1, -1, -1)
    for j in columns:

        @needed(j)
        def _():
            for d in far_first:
                core_out[d, j] = piece(2 * chip_at(d) + 1 - core, j)
                core_copy(d, j).start()

    for k in range(blocks, len(mean_tiles)):
        add_shards(k)

    for j in columns:

        @needed(j)
        def _():
            for d in far_first:
                block = 2 * chip_at(d) + core
                core_copy(d, j).wait_recv()
                theirs = (owner_ref[block] == partner).astype(jnp.int32)
                chosen = jnp.where(
                    jnp.full((rows, LANES), theirs) > 0, core_in[d, j], piece(block, j)
                )
                if d:
                    route_out[d, j] = chosen
                    route_copy(d, j).start()
                else:
                    route_in[chip, j] = chosen

    for a in range(blocks):
        low = a * LANES
        gram = nt_dot(grads_ref[0, 0, low : low + LANES, :], grads_ref[0, 0, low:, :])
        for s in range(1, shards):
            gram = gram + nt_dot(grads_ref[s, 0, low : low + LANES, :], grads_ref[s, 0, low:, :])
        for k, (i, j) in enumerate(stat_tiles):
            if i * rows // LANES == a:
                r = i * rows - low
                loc[early + k] = gram[r : r + rows, j * LANES - low : (j + 1) * LANES - low]

    def inject():
        for j in range(blocks):

            @needed(j)
            def _():
                for d in range(1, chips):
                    route_copy(d, j).wait_recv()

        for k, (i, j) in enumerate(stat_tiles):

            @pl.when(rep == i)
            def _():
                loc[early + k] = loc[early + k] + route_in[owner_ref[pre] // 2, j]

    @pl.when(is_end)
    def _():
        @pl.loop(early, early + free)
        def _(k):
            send_in(k)

        inject()

        @pl.loop(early + free, total)
        def _(k):
            send_in(k)

    @pl.loop(0, LAG)
    def _(k):
        step_up(k)

    @pl.loop(LAG, early)
    def _(k):
        step_up(k)
        step_down(k - LAG)

    @pl.when(not_end)
    def _():
        inject()

    start = pl.multiple_of(rep * rows, rows)

    def rows_copy(d, j):
        device = {"pre": 2 * chip_at(d) + core} if d else {"pre": partner}
        return remote(
            stat.at[pl.ds(start, rows), pl.ds(j * LANES, LANES)],
            rows_in.at[pre, j],
            rows_send.at[d, j],
            rows_recv.at[d, j],
            device,
        )

    def pass_copy(d, j):
        held = rows_in.at[2 * chip_at(d) + core, j]
        return remote(held, held, pass_send.at[d, j], pass_recv.at[d, j], {"pre": partner})

    def pass_on(d, j):
        rows_copy(d, j).wait_recv()
        pass_copy(d, j).start()

    def send_rows(j):
        for d in far_first:
            rows_copy(d, j).start()

    @pl.loop(early, early + LAG)
    def _(k):
        step_up(k)
        step_down(k - LAG)

    for k, (i, j) in enumerate(stat_tiles):
        step_up(early + LAG + k)
        step_down(early + k)
        rs, cs = slice(i * rows, (i + 1) * rows), slice(j * LANES, (j + 1) * LANES)
        stat[rs, cs] = tot[early + k]
        if rows == LANES:

            @pl.when(rep == i)
            def _():
                send_rows(j)

            if i != j:
                stat[cs, rs] = tot[early + k].T

                @pl.when(rep == j)
                def _():
                    send_rows(i)

    if rows != LANES:
        for a in range(blocks):
            for b in range(a + 1, blocks):
                ra, rb = slice(a * LANES, (a + 1) * LANES), slice(b * LANES, (b + 1) * LANES)
                stat[rb, ra] = stat[ra, rb].T
        for j in range(blocks):
            send_rows(j)
    for j in range(blocks):
        rows_in[pre, j] = stat[pl.ds(start, rows), j * LANES : (j + 1) * LANES]

    def pump(part, parts=10):
        left = total - after
        for k in range(left * part // parts, left * (part + 1) // parts):

            @pl.when(not_end)
            def _():
                if after + LAG + k < total:
                    step_up(after + LAG + k)
                step_down(after + k)

    def put_mean(k):
        i, j = mean_tiles[k]
        mean[i * rows : (i + 1) * rows, j * LANES : (j + 1) * LANES] = (
            tot[mean_place(k)] / (shards * n_rep)
        ).astype(jnp.bfloat16)

    pump(0)
    for k in range(early):
        put_mean(k)

    def eye(first, count):
        r = lax.broadcasted_iota(jnp.int32, (count, order), 0) + first
        c = lax.broadcasted_iota(jnp.int32, (count, order), 1)
        return (r == c).astype(jnp.float32)

    bands = range(0, order, 256)
    squares = jnp.zeros((1, 1), jnp.float32)
    for b in bands:
        part = stat[b : b + 256, :]
        squares = squares + jnp.sum(part * part, keepdims=True)
    shift = DAMP * jnp.sqrt(squares)
    squares = jnp.zeros((1, 1), jnp.float32)
    for b in bands:
        part = stat[b : b + 256, :] + shift * eye(b, 256)
        x_f32[b : b + 256, :] = part
        squares = squares + jnp.sum(part * part, keepdims=True)
    scale = jnp.sqrt(squares)
    pump(1)
    for b in bands:
        part = x_f32[b : b + 256, :] / scale
        x_f32[b : b + 256, :] = part
        x_b16[b : b + 256, :] = part.astype(jnp.bfloat16)
    root = (1.25 * eye(start, rows) - 0.25 * x_f32[pl.ds(start, rows), :]) / jnp.sqrt(
        jnp.sqrt(scale)
    )
    pump(2)

    def quadratic(b):
        square = dot(x_b16[pl.ds(b, 256), :], x_b16[...])
        return 0.0625 * square - 0.625 * x_f32[pl.ds(b, 256), :]

    for turn in range(2):

        @pl.loop(0, order, step=256)
        def _(b):
            e = quadratic(b)
            e_f32[pl.ds(b, 256), :] = e
            e_b16[pl.ds(b, 256), :] = e.astype(jnp.bfloat16)

        pump(3 + 3 * turn)

        @pl.loop(0, order, step=256)
        def _(b):
            g = 2.0 * CENTER * e_f32[pl.ds(b, 256), :] + dot(e_b16[pl.ds(b, 256), :], e_b16[...])
            g_b16[pl.ds(b, 256), :] = g.astype(jnp.bfloat16)

        pump(4 + 3 * turn)

        @pl.loop(0, order, step=256)
        def _(b):
            x = CENTER * CENTER * x_f32[pl.ds(b, 256), :] + dot(
                x_b16[pl.ds(b, 256), :], g_b16[...]
            )
            x_f32[pl.ds(b, 256), :] = x
            x_b16[pl.ds(b, 256), :] = x.astype(jnp.bfloat16)

        root = 1.25 * root - 0.25 * dot(root.astype(jnp.bfloat16), x_b16[...])
        pump(5 + 3 * turn)

    for d in range(1, chips - 1):
        for j in range(blocks):
            pass_on(d, j)

    @pl.loop(0, order, step=256)
    def _(b):
        e_b16[pl.ds(b, 256), :] = quadratic(b).astype(jnp.bfloat16)

    last = dot(root.astype(jnp.bfloat16), x_b16[...])
    for _ in range(2):
        last = CENTER * last + dot(last.astype(jnp.bfloat16), e_b16[...])
    precond = (1.25 * root - 0.25 * last).astype(jnp.bfloat16)
    pump(9)
    for j in range(blocks):
        pass_on(chips - 1, j)

    for j in range(blocks):
        rows_copy(0, j).wait_recv()
        for d in range(1, chips):
            pass_copy(d, j).wait_recv()
    for j in range(blocks):
        cs = slice(j * LANES, (j + 1) * LANES)
        for held, at in enumerate((first, second)):
            taken = jnp.full((rows, LANES), count, jnp.int32) > held
            gain_ref[0, held, :, cs] = jnp.where(
                taken, rows_in[at, j] - state_ref[0, held, :, cs], 0.0
            )

    for k in range(early, len(mean_tiles)):

        @pl.when(is_end)
        def _():
            step_down(mean_place(k))

        put_mean(k)
    update_ref[0] = dot(precond, mean[...]).astype(jnp.bfloat16)

    for j in range(blocks):

        @needed(j)
        def _():
            for d in range(chips):
                core_copy(d, j).wait_send()
                if d:
                    route_copy(d, j).wait_send()

        for d in range(chips):
            rows_copy(d, j).wait_send()
            if d:
                pass_copy(d, j).wait_send()

    @pl.loop(0, total)
    def _(k):
        in_copy(k).wait_send()

        @pl.when(not_end)
        def _():
            out_copy(k).wait_send()


def body(n_pre, n_rep, grads, owner, state):
    order = grads.shape[2]
    rows = state.shape[2]
    blocks = order // LANES
    total = n_rep * blocks + sum(blocks - i * rows // LANES for i in range(n_rep))
    f32, b16 = jnp.float32, jnp.bfloat16
    dma = pltpu.SemaphoreType.DMA
    vmem = pl.BlockSpec(memory_space=pltpu.VMEM)
    gain, update = pl.pallas_call(
        functools.partial(kernel, n_pre, n_rep),
        out_shape=(
            jax.ShapeDtypeStruct(state.shape, f32),
            jax.ShapeDtypeStruct((1, rows, order), b16),
        ),
        in_specs=[pl.BlockSpec(memory_space=pltpu.SMEM)]
        + [pl.BlockSpec(memory_space=pltpu.HBM)] * 2,
        out_specs=(vmem, vmem),
        scratch_shapes=[pltpu.VMEM(grads.shape, b16), pltpu.VMEM(state.shape, f32)]
        + [pltpu.VMEM((total, rows, LANES), f32)] * 4
        + [pltpu.VMEM((n_pre // 2, blocks, rows, LANES), f32)] * 4
        + [pltpu.VMEM((n_pre, blocks, rows, LANES), f32)]
        + [pltpu.VMEM((order, order), t) for t in (f32, b16, f32, b16, f32, b16, b16)]
        + [dma((total,))] * 4
        + [dma((n_pre // 2, blocks))] * 8
        + [dma((blocks + 1,))],
        compiler_params=pltpu.CompilerParams(
            collective_id=0, has_side_effects=True, vmem_limit_bytes=60 * 1024 * 1024
        ),
        cost_estimate=pl.CostEstimate(
            flops=20 * order**3, bytes_accessed=4 * order * order * 4, transcendentals=0
        ),
    )(owner, grads, state)
    return state + gain, update


def solution(mesh):
    placed = (P("rep", "pre", None, None), P(), P("pre", None, "rep", None))
    return jax.shard_map(
        functools.partial(body, mesh.shape["pre"], mesh.shape["rep"]),
        mesh=mesh,
        in_specs=placed,
        out_specs=(P("pre", None, "rep", None), P("pre", "rep", None)),
        check_vma=False,
    )
```

```python
import functools

import jax
import jax.numpy as jnp
from jax import lax
from jax.experimental import pallas as pl
from jax.experimental.pallas import tpu as pltpu
from jax.sharding import PartitionSpec as P

DAMP = 0.05
LANES = 128
LAG = 3
CENTER = 1.5625


def nt_dot(a, b):
    return lax.dot_general(a, b, (((1,), (1,)), ((), ())), preferred_element_type=jnp.float32)


def dot(a, b):
    return jnp.dot(a, b, preferred_element_type=jnp.float32)


def kernel(
    n_pre,
    n_rep,
    owner_ref,
    grads_hbm,
    state_hbm,
    new_state_ref,
    update_ref,
    grads_ref,
    state_ref,
    loc,
    up,
    dn,
    tot,
    core_out,
    core_in,
    route_out,
    route_in,
    rows_in,
    stat,
    mean,
    x_f32,
    x_b16,
    e_f32,
    e_b16,
    g_b16,
    in_send,
    out_send,
    up_recv,
    dn_recv,
    core_send,
    core_recv,
    route_send,
    route_recv,
    rows_send,
    rows_recv,
    pass_send,
    pass_recv,
    load_sem,
):
    pre, rep = lax.axis_index("pre"), lax.axis_index("rep")
    shards, order = grads_ref.shape[0], grads_ref.shape[2]
    rows = state_ref.shape[2]
    blocks = order // LANES
    half = n_rep // 2
    is_end = (rep == 0) | (rep == n_rep - 1)
    is_mid = (rep == half - 1) | (rep == half)
    not_end, not_mid = jnp.logical_not(is_end), jnp.logical_not(is_mid)
    inward = jnp.where(rep < half, rep + 1, rep - 1)
    outward = jnp.where(rep < half, rep - 1, rep + 1)
    chips, chip, core = n_pre // 2, pre // 2, pre % 2
    partner = pre + 1 - 2 * core

    def chip_at(d):
        other, bit = chip, 1
        while bit < chips:
            if d & bit:
                other = other + bit * (1 - 2 * ((chip // bit) % 2))
            bit *= 2
        return other

    mean_tiles = [(i, j) for i in range(n_rep) for j in range(blocks)]
    bands_out = sorted(range(n_rep), key=lambda i: abs(2 * i + 1 - n_rep))
    stat_tiles = [(i, j) for i in bands_out for j in range(i * rows // LANES, blocks)]
    free = sum(0 < i < n_rep - 1 for i, _ in stat_tiles)
    early = len(mean_tiles) // 2
    after = early + len(stat_tiles)
    total = len(mean_tiles) + len(stat_tiles)

    def mean_place(k):
        return k if k < early else k + len(stat_tiles)

    def remote(src, dst, send, recv, device):
        return pltpu.make_async_remote_copy(
            src_ref=src,
            dst_ref=dst,
            send_sem=send,
            recv_sem=recv,
            device_id=device,
            device_id_type=pl.DeviceIdType.MESH,
        )

    def load(a):
        band = slice(a * LANES, (a + 1) * LANES)
        return pltpu.make_async_copy(
            grads_hbm.at[:, :, band, :], grads_ref.at[:, :, band, :], load_sem.at[a]
        )

    load_state = pltpu.make_async_copy(state_hbm, state_ref, load_sem.at[blocks])
    load_state.start()
    for a in range(blocks):
        load(a).start()

    count = first = second = jnp.int32(0)
    for b in range(n_pre):
        here = owner_ref[b] == pre
        first = jnp.where(here & (count == 0), b, first)
        second = jnp.where(here & (count == 1), b, second)
        count = count + here.astype(jnp.int32)

    barrier = pltpu.get_barrier_semaphore()

    def greet(device):
        pl.semaphore_signal(
            barrier, inc=1, device_id=device, device_id_type=pl.DeviceIdType.MESH
        )

    for d in range(1, chips):
        greet({"pre": 2 * chip_at(d) + core})
    greet({"pre": partner})
    greet({"rep": inward})

    @pl.when(not_end)
    def _():
        greet({"rep": outward})

    pl.semaphore_wait(barrier, jnp.where(is_end, chips + 1, chips + 2))

    def send_in(k):
        @pl.when(is_mid)
        def _():
            remote(
                loc.at[k], dn.at[k], in_send.at[k], dn_recv.at[k], {"rep": inward}
            ).start()

        @pl.when(not_mid)
        def _():
            remote(
                loc.at[k], up.at[k], in_send.at[k], up_recv.at[k], {"rep": inward}
            ).start()

    def out_copy(k):
        return remote(tot.at[k], dn.at[k], out_send.at[k], dn_recv.at[k], {"rep": outward})

    def in_copy(k):
        return remote(loc.at[k], up.at[k], in_send.at[k], up_recv.at[k], {"rep": inward})

    def step_up(k):
        @pl.when(not_end)
        def _():
            in_copy(k).wait_recv()
            loc[k] = loc[k] + up[k]
            send_in(k)

    def step_down(k):
        out_copy(k).wait_recv()

        @pl.when(is_mid)
        def _():
            tot[k] = loc[k] + dn[k]

        @pl.when(not_mid)
        def _():
            tot[k] = dn[k]

        @pl.when(not_end)
        def _():
            out_copy(k).start()

    def piece(block, j):
        at = ((count > 1) & (second == block)).astype(jnp.int32)
        return state_ref[0, at, :, j * LANES : (j + 1) * LANES]

    def core_copy(d, j):
        return remote(
            core_out.at[d, j],
            core_in.at[d, j],
            core_send.at[d, j],
            core_recv.at[d, j],
            {"pre": partner},
        )

    def route_copy(d, j):
        return remote(
            route_out.at[d, j],
            route_in.at[chip, j],
            route_send.at[d, j],
            route_recv.at[d, j],
            {"pre": 2 * chip_at(d) + core},
        )

    def needed(j):
        return pl.when(rep * rows < (j + 1) * LANES)

    load_state.wait()
    far_first = list(range(chips - 1, -1, -1))
    columns = range(blocks - 1, -1, -1)
    for j in columns:

        @needed(j)
        def _():
            for d in far_first:
                core_out[d, j] = piece(2 * chip_at(d) + 1 - core, j)
                core_copy(d, j).start()

    for k, (i, j) in enumerate(mean_tiles):
        if j == 0 and i * rows % LANES == 0:
            load(i * rows // LANES).wait()
        r, c = slice(i * rows, (i + 1) * rows), slice(j * LANES, (j + 1) * LANES)
        acc = grads_ref[0, 0, r, c].astype(jnp.float32)
        for s in range(1, shards):
            acc = acc + grads_ref[s, 0, r, c].astype(jnp.float32)
        loc[mean_place(k)] = acc
        if k < early:

            @pl.when(is_end)
            def _():
                send_in(k)

    for j in columns:

        @needed(j)
        def _():
            for d in far_first:
                block = 2 * chip_at(d) + core
                core_copy(d, j).wait_recv()
                theirs = (owner_ref[block] == partner).astype(jnp.int32)
                chosen = jnp.where(
                    jnp.full((rows, LANES), theirs) > 0, core_in[d, j], piece(block, j)
                )
                if d:
                    route_out[d, j] = chosen
                    route_copy(d, j).start()
                else:
                    route_in[chip, j] = chosen

    for a in range(blocks):
        low = a * LANES
        gram = nt_dot(grads_ref[0, 0, low : low + LANES, :], grads_ref[0, 0, low:, :])
        for s in range(1, shards):
            gram = gram + nt_dot(grads_ref[s, 0, low : low + LANES, :], grads_ref[s, 0, low:, :])
        for k, (i, j) in enumerate(stat_tiles):
            if i * rows // LANES == a:
                r = i * rows - low
                loc[early + k] = gram[r : r + rows, j * LANES - low : (j + 1) * LANES - low]

    def inject():
        for j in range(blocks):

            @needed(j)
            def _():
                for d in range(1, chips):
                    route_copy(d, j).wait_recv()

        for k, (i, j) in enumerate(stat_tiles):

            @pl.when(rep == i)
            def _():
                loc[early + k] = loc[early + k] + route_in[owner_ref[pre] // 2, j]

    @pl.when(is_end)
    def _():
        @pl.loop(early, early + free)
        def _(k):
            send_in(k)

        inject()

        @pl.loop(early + free, total)
        def _(k):
            send_in(k)

    @pl.loop(0, LAG)
    def _(k):
        step_up(k)

    @pl.loop(LAG, early)
    def _(k):
        step_up(k)
        step_down(k - LAG)

    @pl.when(not_end)
    def _():
        inject()

    start = pl.multiple_of(rep * rows, rows)

    def rows_copy(d, j):
        device = {"pre": 2 * chip_at(d) + core} if d else {"pre": partner}
        return remote(
            stat.at[pl.ds(start, rows), pl.ds(j * LANES, LANES)],
            rows_in.at[pre, j],
            rows_send.at[d, j],
            rows_recv.at[d, j],
            device,
        )

    def pass_copy(d, j):
        held = rows_in.at[2 * chip_at(d) + core, j]
        return remote(held, held, pass_send.at[d, j], pass_recv.at[d, j], {"pre": partner})

    def pass_on(d, j):
        rows_copy(d, j).wait_recv()
        pass_copy(d, j).start()

    def send_rows(j):
        for d in far_first:
            rows_copy(d, j).start()

    @pl.loop(early, early + LAG)
    def _(k):
        step_up(k)
        step_down(k - LAG)

    for k, (i, j) in enumerate(stat_tiles):
        step_up(early + LAG + k)
        step_down(early + k)
        rs, cs = slice(i * rows, (i + 1) * rows), slice(j * LANES, (j + 1) * LANES)
        stat[rs, cs] = tot[early + k]
        if rows == LANES:

            @pl.when(rep == i)
            def _():
                send_rows(j)

            if i != j:
                stat[cs, rs] = tot[early + k].T

                @pl.when(rep == j)
                def _():
                    send_rows(i)

    if rows != LANES:
        for a in range(blocks):
            for b in range(a + 1, blocks):
                ra, rb = slice(a * LANES, (a + 1) * LANES), slice(b * LANES, (b + 1) * LANES)
                stat[rb, ra] = stat[ra, rb].T
        for j in range(blocks):
            send_rows(j)
    for j in range(blocks):
        rows_in[pre, j] = stat[pl.ds(start, rows), j * LANES : (j + 1) * LANES]

    def pump(part, parts=10):
        left = total - after
        for k in range(left * part // parts, left * (part + 1) // parts):

            @pl.when(not_end)
            def _():
                if after + LAG + k < total:
                    step_up(after + LAG + k)
                step_down(after + k)

    pump(0)

    def eye(first, count):
        r = lax.broadcasted_iota(jnp.int32, (count, order), 0) + first
        c = lax.broadcasted_iota(jnp.int32, (count, order), 1)
        return (r == c).astype(jnp.float32)

    bands = range(0, order, 256)
    squares = jnp.zeros((1, 1), jnp.float32)
    for b in bands:
        part = stat[b : b + 256, :]
        squares = squares + jnp.sum(part * part, keepdims=True)
    shift = DAMP * jnp.sqrt(squares)
    squares = jnp.zeros((1, 1), jnp.float32)
    for b in bands:
        part = stat[b : b + 256, :] + shift * eye(b, 256)
        x_f32[b : b + 256, :] = part
        squares = squares + jnp.sum(part * part, keepdims=True)
    scale = jnp.sqrt(squares)
    pump(1)
    for b in bands:
        part = x_f32[b : b + 256, :] / scale
        x_f32[b : b + 256, :] = part
        x_b16[b : b + 256, :] = part.astype(jnp.bfloat16)
    root = (1.25 * eye(start, rows) - 0.25 * x_f32[pl.ds(start, rows), :]) / jnp.sqrt(
        jnp.sqrt(scale)
    )
    pump(2)

    def quadratic(b):
        square = dot(x_b16[pl.ds(b, 256), :], x_b16[...])
        return 0.0625 * square - 0.625 * x_f32[pl.ds(b, 256), :]

    for turn in range(2):

        @pl.loop(0, order, step=256)
        def _(b):
            e = quadratic(b)
            e_f32[pl.ds(b, 256), :] = e
            e_b16[pl.ds(b, 256), :] = e.astype(jnp.bfloat16)

        pump(3 + 3 * turn)

        @pl.loop(0, order, step=256)
        def _(b):
            g = 2.0 * CENTER * e_f32[pl.ds(b, 256), :] + dot(e_b16[pl.ds(b, 256), :], e_b16[...])
            g_b16[pl.ds(b, 256), :] = g.astype(jnp.bfloat16)

        pump(4 + 3 * turn)

        @pl.loop(0, order, step=256)
        def _(b):
            x = CENTER * CENTER * x_f32[pl.ds(b, 256), :] + dot(
                x_b16[pl.ds(b, 256), :], g_b16[...]
            )
            x_f32[pl.ds(b, 256), :] = x
            x_b16[pl.ds(b, 256), :] = x.astype(jnp.bfloat16)

        root = 1.25 * root - 0.25 * dot(root.astype(jnp.bfloat16), x_b16[...])
        pump(5 + 3 * turn)

    for d in range(1, chips - 1):
        for j in range(blocks):
            pass_on(d, j)

    @pl.loop(0, order, step=256)
    def _(b):
        e_b16[pl.ds(b, 256), :] = quadratic(b).astype(jnp.bfloat16)

    last = dot(root.astype(jnp.bfloat16), x_b16[...])
    for _ in range(2):
        last = CENTER * last + dot(last.astype(jnp.bfloat16), e_b16[...])
    precond = (1.25 * root - 0.25 * last).astype(jnp.bfloat16)
    pump(9)
    for j in range(blocks):
        pass_on(chips - 1, j)

    @pl.when(is_end)
    def _():
        @pl.loop(after, total)
        def _(k):
            step_down(k)

    for k, (i, j) in enumerate(mean_tiles):
        mean[i * rows : (i + 1) * rows, j * LANES : (j + 1) * LANES] = (
            tot[mean_place(k)] / (shards * n_rep)
        ).astype(jnp.bfloat16)
    update_ref[0] = dot(precond, mean[...]).astype(jnp.bfloat16)

    for j in range(blocks):
        rows_copy(0, j).wait_recv()
        for d in range(1, chips):
            pass_copy(d, j).wait_recv()
    for j in range(blocks):
        cs = slice(j * LANES, (j + 1) * LANES)
        for held, at in enumerate((first, second)):
            taken = jnp.full((rows, LANES), count, jnp.int32) > held
            new_state_ref[0, held, :, cs] = jnp.where(
                taken, rows_in[at, j], state_ref[0, held, :, cs]
            )

    for j in range(blocks):

        @needed(j)
        def _():
            for d in range(chips):
                core_copy(d, j).wait_send()
                if d:
                    route_copy(d, j).wait_send()

        for d in range(chips):
            rows_copy(d, j).wait_send()
            if d:
                pass_copy(d, j).wait_send()

    @pl.loop(0, total)
    def _(k):
        in_copy(k).wait_send()

        @pl.when(not_end)
        def _():
            out_copy(k).wait_send()


def body(n_pre, n_rep, grads, owner, state):
    order = grads.shape[2]
    rows = state.shape[2]
    blocks = order // LANES
    total = n_rep * blocks + sum(blocks - i * rows // LANES for i in range(n_rep))
    f32, b16 = jnp.float32, jnp.bfloat16
    dma = pltpu.SemaphoreType.DMA
    vmem = pl.BlockSpec(memory_space=pltpu.VMEM)
    return pl.pallas_call(
        functools.partial(kernel, n_pre, n_rep),
        out_shape=(
            jax.ShapeDtypeStruct(state.shape, f32),
            jax.ShapeDtypeStruct((1, rows, order), b16),
        ),
        in_specs=[pl.BlockSpec(memory_space=pltpu.SMEM)]
        + [pl.BlockSpec(memory_space=pltpu.HBM)] * 2,
        out_specs=(vmem, vmem),
        scratch_shapes=[pltpu.VMEM(grads.shape, b16), pltpu.VMEM(state.shape, f32)]
        + [pltpu.VMEM((total, rows, LANES), f32)] * 4
        + [pltpu.VMEM((n_pre // 2, blocks, rows, LANES), f32)] * 4
        + [pltpu.VMEM((n_pre, blocks, rows, LANES), f32)]
        + [pltpu.VMEM((order, order), t) for t in (f32, b16, f32, b16, f32, b16, b16)]
        + [dma((total,))] * 4
        + [dma((n_pre // 2, blocks))] * 8
        + [dma((blocks + 1,))],
        compiler_params=pltpu.CompilerParams(
            collective_id=0, has_side_effects=True, vmem_limit_bytes=40 * 1024 * 1024
        ),
        cost_estimate=pl.CostEstimate(
            flops=20 * order**3, bytes_accessed=4 * order * order * 4, transcendentals=0
        ),
    )(
        pltpu.with_memory_space_constraint(owner, pltpu.HBM),
        pltpu.with_memory_space_constraint(grads, pltpu.HBM),
        pltpu.with_memory_space_constraint(state, pltpu.HBM),
    )


def solution(mesh):
    placed = (P("rep", "pre", None, None), P(), P("pre", None, "rep", None))
    return jax.shard_map(
        functools.partial(body, mesh.shape["pre"], mesh.shape["rep"]),
        mesh=mesh,
        in_specs=placed,
        out_specs=(P("pre", None, "rep", None), P("pre", "rep", None)),
        check_vma=False,
    )
```
